32 devices in a mesh: energy: 8 (over y, x, core), slab: 4 (over z).
Axes of the slice: x: 2, y: 2, z: 4, core: 2. Of those that a mesh axis runs over, the one named last changes fastest.
Arguments:
- hamiltonian: float32 [4, 2, 256, 256], P('slab'), may hold values from -1 to 1, as said below
- contact: float32 [2, 8, 2, 2, 256, 256], P(None, 'energy'), may hold values from -0.109375 to 0.109375
- hop: float32 [3, 256], replicated, may hold values from 0.4 to 1.2
- bond: int32 [3, 256], replicated, may hold values from 0 to 255, each once within a row
- shifts: int32 [4], replicated, may hold values from -3 to 3, as said below
- strength: float32 [4], replicated, may hold values from 0.1 to 0.4
- coupling: float32 [256, 256], replicated, may hold values from -0.375 to 0.375
Outputs:
- green: float32 [2, 8, 4, 2, 256, 256], P(None, 'energy', 'slab')
- self_energy: float32 [2, 8, 4, 2, 256, 256], P(None, 'energy', 'slab')
- density: float32 [4, 256], P('slab')
The draws below stay inside these ranges and needn't reach their ends.
Inputs may be any that keep to these rules, and one draw needn't show every extreme that they name: `hamiltonian`: each slab's block is Hermitian: the real part symmetric, the imaginary part antisymmetric with a zero diagonal. `shifts`: the table is 3, -3, k, -k in this order, for some k with 1 <= k < 3.
All inputs are finite; a program needn't handle non-finite values.
Results may differ from the reference program's by a relative error of at most 0.0001.
Values sent between devices are 32-bit elements; how exact they have to be, the bound alone decides.
A program may use at most 128 MiB of HBM per device.

```python
import math
import jax
import jax.numpy as jnp
from jax import lax

B = 256
EROWS = 2
ITERS = 1
NEWTON = 2
MODES = 4
KMAX = 3
SLABS = 4
ECOLS = 8
ENERGIES = 16


def draw_hamiltonian(key, part):
    subkeys = jax.random.split(key, 3)
    block_shape = (SLABS, B, B)
    noise_real = jnp.clip(0.03 * jax.random.normal(subkeys[0], block_shape, jnp.float32), -0.15, 0.15)
    noise_imag = jnp.clip(0.03 * jax.random.normal(subkeys[1], block_shape, jnp.float32), -0.15, 0.15)
    onsite = jax.random.uniform(subkeys[2], (SLABS, B), jnp.float32, -0.4, 0.4)
    identity = jnp.eye(B, dtype=jnp.float32)
    symmetric = 0.7071 * (noise_real + jnp.swapaxes(noise_real, 1, 2))
    skew_part = 0.7071 * (noise_imag - jnp.swapaxes(noise_imag, 1, 2))
    real_part = symmetric * (1.0 - identity) + onsite[:, :, None] * identity
    return jnp.stack([real_part, skew_part], axis=1)


def draw_shifts(key, part):
    second = jax.random.randint(key, (), 1, KMAX, dtype=jnp.int32)
    largest = jnp.full((), KMAX, dtype=jnp.int32)
    return jnp.stack([largest, -largest, second, -second]).astype(jnp.int32)


def levels(rng, dims, pieces, low, high):
    def one(dim, blocks):
        steps = jax.random.uniform(jax.random.fold_in(jax.random.fold_in(rng, 6), dim), (blocks,), jnp.float32, low / len(pieces), high / len(pieces))
        return jnp.repeat(jnp.exp(steps), dims[dim] // blocks).reshape((-1,) + (1,) * (len(dims) - dim - 1))

    gain = one(*pieces[0])
    for cut in pieces[1:]:
        gain = gain * one(*cut)
    return gain


def gaussian(own_key, extent, scale, limit, pieces=(), kind=jnp.bfloat16):
    array = scale * jax.random.normal(own_key, extent, jnp.float32)
    if pieces:
        array = array * levels(own_key, extent, pieces, -0.22, 0.18)
    return jnp.clip(array, -limit, limit).astype(kind)


def setup_inputs(seed: int = 0) -> dict:
    key_of = jax.random.split(jax.random.key(seed), 8)
    return {
        "hamiltonian": draw_hamiltonian(jax.random.fold_in(key_of[7], 71), 0),
        "contact": gaussian(key_of[1], (EROWS, ECOLS, 2, 2, B, B), (11 * B) ** -0.5, 0.109375, ((1, 8),), jnp.float32),
        "hop": jnp.clip(jnp.exp(jax.random.uniform(key_of[2], (SLABS - 1, B), jnp.float32, math.log(0.4), math.log(1.2))), 0.4, 1.2),
        "bond": jax.vmap(lambda own: jax.random.permutation(own, B))(jax.random.split(key_of[3], (SLABS - 1))).reshape((SLABS - 1, B)).astype(jnp.int32),
        "shifts": draw_shifts(jax.random.fold_in(key_of[7], 71), 0),
        "strength": jnp.clip(jnp.exp(jax.random.uniform(key_of[5], (MODES,), jnp.float32, math.log(0.1), math.log(0.4))), 0.1, 0.4),
        "coupling": gaussian(key_of[6], (B, B), B ** -0.5, 0.375, (), jnp.float32),
    }


PRECISE = lax.Precision.HIGHEST
BROADENING = 0.5
ENERGY_LOW = 4.0
ENERGY_SPAN = 1.0


def complex_product(left_block, right_block):
    real_part = jnp.matmul(left_block[..., 0, :, :], right_block[..., 0, :, :], precision=PRECISE) - jnp.matmul(left_block[..., 1, :, :], right_block[..., 1, :, :], precision=PRECISE)
    imag_part = jnp.matmul(left_block[..., 0, :, :], right_block[..., 1, :, :], precision=PRECISE) + jnp.matmul(left_block[..., 1, :, :], right_block[..., 0, :, :], precision=PRECISE)
    return jnp.stack([real_part, imag_part], axis=-3)


def left_real_part(matrix, matrix_blocks):
    return jnp.einsum("ab,...bc->...ac", matrix, matrix_blocks, precision=PRECISE)


def right_real_part(matrix_blocks, matrix):
    return jnp.einsum("...ab,bc->...ac", matrix_blocks, matrix, precision=PRECISE)


def complement_term(matrix_blocks, forward_state):
    return right_real_part(left_real_part(forward_state.T, matrix_blocks), forward_state)


def expansion_term(matrix_blocks, forward_state):
    return right_real_part(left_real_part(forward_state, matrix_blocks), forward_state.T)


def invert(matrix_blocks):
    orbitals = matrix_blocks.shape[-1]
    identity = jnp.eye(orbitals, dtype=jnp.float32)
    diag_re = jnp.diagonal(matrix_blocks[..., 0, :, :], axis1=-2, axis2=-1)
    diag_im = jnp.diagonal(matrix_blocks[..., 1, :, :], axis1=-2, axis2=-1)
    modulus = diag_re * diag_re + diag_im * diag_im
    approx = jnp.stack([(diag_re / modulus)[..., None, :] * identity, (-diag_im / modulus)[..., None, :] * identity], axis=-3)
    doubled = jnp.stack([2.0 * identity, jnp.zeros_like(identity)])
    for newton_step in range(NEWTON):
        approx = complex_product(approx, doubled - complex_product(matrix_blocks, approx))
    return approx


def green_blocks(hamiltonian, contact, self_energy, couplers, energy):
    orbitals = hamiltonian.shape[-1]
    count = energy.shape[0]
    identity = jnp.eye(orbitals, dtype=jnp.float32)
    base_diag = jnp.stack([energy[:, None, None] * identity, jnp.broadcast_to(BROADENING * identity, (count, orbitals, orbitals))], axis=1)
    matrix_blocks = []
    for slab in range(SLABS):
        block = base_diag - hamiltonian[slab] - self_energy[:, slab]
        if slab == 0:
            block = block - contact[:, 0]
        if slab == SLABS - 1:
            block = block - contact[:, 1]
        matrix_blocks.append(block)
    half = SLABS // 2
    left_green = []
    left_reduced = []
    forwarded_value = jnp.zeros_like(matrix_blocks[0])
    for slab in range(half):
        reduced = matrix_blocks[slab] - forwarded_value
        inverse_matrix = invert(reduced)
        left_reduced.append(reduced)
        left_green.append(inverse_matrix)
        forwarded_value = complement_term(inverse_matrix, couplers[slab])
    right_green = {}
    right_reduced = {}
    carried_right = jnp.zeros_like(matrix_blocks[0])
    for slab in range(SLABS - 1, half - 1, -1):
        reduced = matrix_blocks[slab] - carried_right
        inverse_matrix = invert(reduced)
        right_reduced[slab] = reduced
        right_green[slab] = inverse_matrix
        carried_right = expansion_term(inverse_matrix, couplers[slab - 1])
    final_output = [None] * SLABS
    final_output[half - 1] = invert(left_reduced[-1] - carried_right)
    final_output[half] = invert(right_reduced[half] - forwarded_value)
    for slab in range(half - 2, -1, -1):
        interior_term = expansion_term(final_output[slab + 1], couplers[slab])
        factor = left_green[slab]
        final_output[slab] = factor + complex_product(complex_product(factor, interior_term), factor)
    for slab in range(half + 1, SLABS):
        interior_term = complement_term(final_output[slab - 1], couplers[slab - 1])
        factor = right_green[slab]
        final_output[slab] = factor + complex_product(complex_product(factor, interior_term), factor)
    return jnp.stack(final_output, axis=1)


def phonon_term(green, shifts, strength, coupling):
    count = green.shape[0]
    positions = jnp.arange(count, dtype=jnp.int32)
    accum = jnp.zeros_like(green)
    for mode in range(MODES):
        source = (positions + shifts[mode]).astype(jnp.int32)
        inside = jnp.logical_and(source >= 0, source < count)
        picked = jnp.take(green, jnp.clip(source, 0, count - 1).astype(jnp.int32), axis=0)
        accum = accum + jnp.where(inside[:, None, None, None, None], strength[mode] * picked, 0.0)
    return right_real_part(left_real_part(coupling, accum), coupling.T)


def reference(hamiltonian, contact, hop, bond, shifts, strength, coupling):
    orbitals = hamiltonian.shape[-1]
    energy = ENERGY_LOW + ENERGY_SPAN * jnp.arange(ENERGIES, dtype=jnp.int32).astype(jnp.float32) / ENERGIES
    energy_rows = energy.reshape(EROWS, ECOLS)
    columns = jnp.arange(orbitals, dtype=jnp.int32)
    couplers = [hop[k][:, None] * (bond[k][:, None] == columns[None, :]).astype(jnp.float32) for k in range(SLABS - 1)]
    self_energy = jnp.zeros((ENERGIES, SLABS, 2, orbitals, orbitals), jnp.float32)
    green = self_energy

    def row_solve(packed):
        return green_blocks(hamiltonian, packed[0], packed[1], couplers, packed[2])

    for born_step in range(ITERS):
        table_self = self_energy.reshape(EROWS, ECOLS, SLABS, 2, orbitals, orbitals)
        green = lax.map(row_solve, (contact, table_self, energy_rows)).reshape(ENERGIES, SLABS, 2, orbitals, orbitals)
        self_energy = phonon_term(green, shifts, strength, coupling)
    occupation = 1.0 / (1.0 + jnp.exp(3.0 * (energy - (ENERGY_LOW + 0.5 * ENERGY_SPAN))))
    density = jnp.sum(occupation[:, None, None] * (-jnp.diagonal(green[:, :, 1], axis1=-2, axis2=-1)), axis=0)
    green_table = green.reshape(EROWS, ECOLS, SLABS, 2, orbitals, orbitals)
    self_table = self_energy.reshape(EROWS, ECOLS, SLABS, 2, orbitals, orbitals)
    return green_table, self_table, density
```

```python
import functools
import math

import jax
import jax.numpy as jnp
from jax import lax
from jax.experimental import pallas as pl
from jax.experimental.pallas import tpu as pltpu
from jax.sharding import PartitionSpec as P

KMAX = 3
BROADENING = 0.5
ENERGY_LOW = 4.0
ENERGY_SPAN = 1.0
MESH = pl.DeviceIdType.MESH
VMEM_LIMIT = 56 * 1024 * 1024
F32 = jnp.float32
BF16 = jnp.bfloat16


def iotas(shape):
    return (
        lax.broadcasted_iota(jnp.int32, shape, 0),
        lax.broadcasted_iota(jnp.int32, shape, 1),
    )


def split(x):
    high = x.astype(BF16)
    return high, (x - high.astype(F32)).astype(BF16)


def dot(a, b):
    return jnp.dot(a, b, preferred_element_type=F32)


def product(a, b):
    size = a[0].shape[-1]
    ar, al = split(a[0])
    ai, am = split(a[1])
    br, bl = split(b[0])
    bi, bm = split(b[1])
    left = jnp.concatenate([ar, al, ar, ai, am, ai], axis=1)
    real = jnp.concatenate([br, br, bl, -bi, -bi, -bm], axis=0)
    imag = jnp.concatenate([bi, bi, bm, br, br, bl], axis=0)
    return dot(left, real), dot(left, imag)


def invert(x):
    size = x[0].shape[-1]
    rows, cols = iotas((size, size))
    eye = rows == cols
    out = []
    recips = []
    for axis in (0, 1):
        dr = jnp.sum(jnp.where(eye, x[0], 0.0), axis=axis, keepdims=True)
        di = jnp.sum(jnp.where(eye, x[1], 0.0), axis=axis, keepdims=True)
        modulus = dr * dr + di * di
        recips.append((dr / modulus, -di / modulus))
    (cr, ci), (rr, ri) = recips
    pr = x[0] * cr - x[1] * ci
    pi = x[0] * ci + x[1] * cr
    qr = jnp.where(eye, 2.0, 0.0) - pr
    qi = -pi
    first = (rr * qr - ri * qi, rr * qi + ri * qr)
    yr, yi = product(x, first)
    return product(first, (jnp.where(eye, 2.0, 0.0) - yr, -yi))


def conjugate(x, coupler):
    left, right, scale_col, scale_row = coupler
    size = left.shape[0]
    hr, lr = split(x[0])
    hi, li = split(x[1])
    moved = dot(left, jnp.concatenate([hr, hi, lr, li], axis=1)).astype(BF16)
    stacked = jnp.concatenate([moved[:, i * size : (i + 1) * size] for i in range(4)], axis=0)
    full = dot(stacked, right)
    real = (full[:size] + full[2 * size : 3 * size]) * scale_col * scale_row
    imag = (full[size : 2 * size] + full[3 * size :]) * scale_col * scale_row
    return real, imag


def gather_kernel(slabs, columns, ham_ref, hall_ref, send1, recv1, send2, recv2):
    column = lax.axis_index("energy")
    slab = lax.axis_index("slab")
    size = ham_ref.shape[-1]
    depth = size // columns
    rows, cols = iotas((size, size))

    barrier = pltpu.get_barrier_semaphore()
    for dz in range(1, slabs):
        pl.semaphore_signal(
            barrier, inc=1, device_id=(column, lax.rem(slab + dz, slabs)), device_id_type=MESH
        )
    for dc in range(1, columns):
        pl.semaphore_signal(
            barrier, inc=1, device_id=(lax.rem(column + dc, columns), slab), device_id_type=MESH
        )
    hall_ref[slab] = jnp.where(rows <= cols, ham_ref[0], ham_ref[1])
    pl.semaphore_wait(barrier, slabs - 1 + columns - 1)

    own = pl.ds(pl.multiple_of(column * depth, depth), depth)

    def along(dz):
        return pltpu.make_async_remote_copy(
            src_ref=hall_ref.at[slab, own],
            dst_ref=hall_ref.at[slab, own],
            send_sem=send1.at[dz],
            recv_sem=recv1.at[dz],
            device_id=(column, lax.rem(slab + dz, slabs)),
            device_id_type=MESH,
        )

    def arrived_along(dz):
        source = lax.rem(slab - dz + slabs, slabs)
        return pltpu.make_async_remote_copy(
            src_ref=hall_ref.at[source, own],
            dst_ref=hall_ref.at[source, own],
            send_sem=send1.at[dz],
            recv_sem=recv1.at[dz],
            device_id=(column, source),
            device_id_type=MESH,
        )

    def across(dz, dc):
        source = lax.rem(slab - dz + slabs, slabs)
        return pltpu.make_async_remote_copy(
            src_ref=hall_ref.at[source, own],
            dst_ref=hall_ref.at[source, own],
            send_sem=send2.at[dz, dc],
            recv_sem=recv2.at[dz, dc],
            device_id=(lax.rem(column + dc, columns), slab),
            device_id_type=MESH,
        )

    def arrived_across(dz, dc):
        source = lax.rem(slab - dz + slabs, slabs)
        partner = lax.rem(column - dc + columns, columns)
        theirs = pl.ds(pl.multiple_of(partner * depth, depth), depth)
        return pltpu.make_async_remote_copy(
            src_ref=hall_ref.at[source, theirs],
            dst_ref=hall_ref.at[source, theirs],
            send_sem=send2.at[dz, dc],
            recv_sem=recv2.at[dz, dc],
            device_id=(partner, slab),
            device_id_type=MESH,
        )

    for dz in range(1, slabs):
        along(dz).start()
    for dz in range(1, slabs):
        arrived_along(dz).wait_recv()
        for dc in range(1, columns):
            across(dz, dc).start()
    for dz in range(1, slabs):
        for dc in range(1, columns):
            arrived_across(dz, dc).wait_recv()
    for dz in range(1, slabs):
        along(dz).wait_send()
        for dc in range(1, columns):
            across(dz, dc).wait_send()


def chain_kernel(slabs, columns, hall_ref, contact_ref, hop_ref, bond_ref, green_ref):
    column = lax.axis_index("energy")
    slab = lax.axis_index("slab")
    row_count = contact_ref.shape[0]
    size = hall_ref.shape[-1]
    half = slabs // 2
    is_left = slab < half
    rows, cols = iotas((size, size))
    eye = rows == cols

    def choose(left, right):
        return jnp.where(is_left, left, right)

    def coupler(k, down):
        bond = bond_ref[pl.ds(k, 1), :]
        hop_row = hop_ref[pl.ds(k, 1), :]
        hop_col = jnp.sum(jnp.where(eye, hop_row, 0.0), axis=1, keepdims=True)
        turned = jnp.where(rows == bond, 1.0, 0.0).astype(F32)
        plain = turned.T
        moved_col = jnp.sum(turned * hop_row, axis=1, keepdims=True)
        moved_row = jnp.sum(plain * hop_col, axis=0, keepdims=True)
        up = (plain.astype(BF16), turned.astype(BF16), hop_col, hop_row)
        lower = (turned.astype(BF16), plain.astype(BF16), moved_col, moved_row)
        flag = down.astype(F32)
        inner = [
            (flag * d.astype(F32) + (1.0 - flag) * u.astype(F32)).astype(u.dtype)
            for d, u in zip(lower[:2], up[:2])
        ]
        scales = [jnp.where(down, d, u) for d, u in zip(lower[2:], up[2:])]
        reverse = [jnp.where(down, u, d) for d, u in zip(lower[2:], up[2:])]
        return tuple(inner + scales), tuple(inner[::-1] + reverse)

    def onsite(index):
        packed = hall_ref[index]
        turned = packed.T
        real = jnp.where(rows <= cols, packed, turned)
        imag = jnp.where(rows > cols, packed, jnp.where(rows < cols, -turned, 0.0))
        return real, imag

    last = slabs - 1
    near_index, far_index = choose(0, last), choose(last, 0)
    near_ham, far_ham = onsite(near_index), onsite(far_index)
    mid_ham = onsite(choose(half - 1, half))
    cross_ham = onsite(choose(half, half - 1))
    near_side, near_back = coupler(choose(0, last - 1), is_left)
    far_side, _ = coupler(choose(last - 1, 0), jnp.logical_not(is_left))
    cross_side, _ = coupler(half - 1, jnp.logical_not(is_left))

    def base(r, ham):
        position = (r * columns + column).astype(F32)
        energy = ENERGY_LOW + ENERGY_SPAN * position / (row_count * columns)
        return (
            jnp.where(eye, energy, 0.0) - ham[0],
            jnp.where(eye, BROADENING, 0.0) - ham[1],
        )

    def minus(a, b):
        return a[0] - b[0], a[1] - b[1]

    span = range(row_count)
    near_end, far_end = choose(0, 1), choose(1, 0)
    near = [
        invert(minus(base(r, near_ham), (contact_ref[r, near_end, 0], contact_ref[r, near_end, 1])))
        for r in span
    ]
    far = [
        invert(minus(base(r, far_ham), (contact_ref[r, far_end, 0], contact_ref[r, far_end, 1])))
        for r in span
    ]
    reduced = [minus(base(r, mid_ham), conjugate(near[r], near_side)) for r in span]
    opposite = [invert(minus(base(r, cross_ham), conjugate(far[r], far_side))) for r in span]
    green = [invert(minus(reduced[r], conjugate(opposite[r], cross_side))) for r in span]
    for r in span:
        green_ref[r, 0] = green[r][0]
        green_ref[r, 1] = green[r][1]

    @pl.when(jnp.logical_or(slab == 0, slab == last))
    def _():
        for r in span:
            inner = conjugate((green_ref[r, 0], green_ref[r, 1]), near_back)
            change = product(product(near[r], inner), near[r])
            green_ref[r, 0] = near[r][0] + change[0]
            green_ref[r, 1] = near[r][1] + change[1]


def phonon_kernel(
    columns, shifts_ref, strength_ref, green_ref, summed_ref, density_ref,
    taken, mixed, shares, send1, recv1, send2, recv2, send3, recv3,
):
    column = lax.axis_index("energy")
    slab = lax.axis_index("slab")
    row_count = green_ref.shape[0]
    size = green_ref.shape[-1]
    depth = size // columns
    count = row_count * columns

    def partner(dc):
        return lax.rem(column + dc + columns, columns)

    def part(index):
        return pl.ds(pl.multiple_of(index * depth, depth), depth)

    barrier = pltpu.get_barrier_semaphore()
    for dc in range(1, columns):
        pl.semaphore_signal(barrier, inc=1, device_id=(partner(dc), slab), device_id_type=MESH)
    taken[:, column] = green_ref[:, :, part(column), :]
    pl.semaphore_wait(barrier, columns - 1)

    def copy(source, target, send, recv, dc, other):
        return pltpu.make_async_remote_copy(
            src_ref=source, dst_ref=target, send_sem=send.at[dc], recv_sem=recv.at[dc],
            device_id=(other, slab), device_id_type=MESH,
        )

    def outward(dc):
        other = partner(dc)
        return copy(
            green_ref.at[:, :, part(other), :], taken.at[:, column], send1, recv1, dc, other
        )

    def outward_in(dc):
        other = partner(-dc)
        return copy(
            green_ref.at[:, :, part(other), :], taken.at[:, other], send1, recv1, dc, other
        )

    def homeward(dc):
        other = partner(dc)
        return copy(
            mixed.at[:, other], summed_ref.at[:, :, part(column), :], send2, recv2, dc, other
        )

    def homeward_in(dc):
        other = partner(-dc)
        return copy(
            mixed.at[:, other], summed_ref.at[:, :, part(other), :], send2, recv2, dc, other
        )

    def share(dc):
        return copy(shares.at[column], shares.at[column], send3, recv3, dc, partner(dc))

    def share_in(dc):
        other = partner(-dc)
        return copy(shares.at[other], shares.at[other], send3, recv3, dc, other)

    others = range(1, columns)
    for dc in others:
        outward(dc).start()
    weights = {}
    for d in range(-KMAX, KMAX + 1):
        if d != 0:
            weights[d] = sum(
                jnp.where(shifts_ref[m] == d, strength_ref[m], 0.0)
                for m in range(shifts_ref.shape[0])
            )
    for dc in others:
        outward_in(dc).wait_recv()

    for e in range(count):
        r, c = divmod(e, columns)
        total = None
        for d, weight in weights.items():
            if 0 <= e + d < count:
                term = weight * taken[(e + d) // columns, (e + d) % columns]
                total = term if total is None else total + term
        mixed[r, c] = total
    for dc in others:
        homeward(dc).start()

    levels = jnp.zeros((depth, size), F32)
    for e in range(count):
        energy = ENERGY_LOW + ENERGY_SPAN * e / count
        occupation = 1.0 / (1.0 + math.exp(3.0 * (energy - (ENERGY_LOW + 0.5 * ENERGY_SPAN))))
        levels = levels - occupation * taken[e // columns, e % columns, 1]
    local_rows, local_cols = iotas((depth, size))
    diagonal = jnp.where(local_rows + column * depth == local_cols, levels, 0.0)
    own_share = jnp.sum(diagonal, axis=0, keepdims=True)
    shares[column] = jnp.broadcast_to(own_share, (8, size))
    for dc in others:
        share(dc).start()

    summed_ref[:, :, part(column), :] = mixed[:, column]
    for dc in others:
        share_in(dc).wait_recv()
    density_ref[...] = jnp.sum(shares[...], axis=0)[:1]
    for dc in others:
        homeward_in(dc).wait_recv()
    for dc in others:
        outward(dc).wait_send()
        homeward(dc).wait_send()
        share(dc).wait_send()


def coupling_kernel(summed_ref, coupling_ref, out_ref):
    size = coupling_ref.shape[0]
    high, low = split(coupling_ref[...])
    left = jnp.concatenate([high, low, high], axis=1)
    right_high, right_low = split(coupling_ref[...].T)
    right = jnp.concatenate([right_high, right_high, right_low], axis=0)
    for r in range(summed_ref.shape[0]):
        for part in range(2):
            a, b = split(summed_ref[r, part])
            half = dot(left, jnp.concatenate([a, a, b], axis=0))
            a, b = split(half)
            out_ref[r, part] = dot(jnp.concatenate([a, b, a], axis=1), right)


def whole():
    return pl.BlockSpec(memory_space=pltpu.VMEM)


def scalar():
    return pl.BlockSpec(memory_space=pltpu.SMEM)


def per_device(slabs, columns, hamiltonian, contact, hop, bond, shifts, strength, coupling):
    size = hamiltonian.shape[-1]
    row_count = contact.shape[0]
    depth = size // columns
    dma = pltpu.SemaphoreType.DMA
    hall = pl.pallas_call(
        functools.partial(gather_kernel, slabs, columns),
        out_shape=jax.ShapeDtypeStruct((slabs, size, size), F32),
        in_specs=[whole()],
        out_specs=whole(),
        scratch_shapes=[
            dma((slabs,)), dma((slabs,)), dma((slabs, columns)), dma((slabs, columns))
        ],
        compiler_params=pltpu.CompilerParams(
            collective_id=0, has_side_effects=True, vmem_limit_bytes=VMEM_LIMIT
        ),
        name="gather_hamiltonian",
    )(hamiltonian[0])
    block = jax.ShapeDtypeStruct((row_count, 2, size, size), F32)
    green = pl.pallas_call(
        functools.partial(chain_kernel, slabs, columns),
        out_shape=block,
        in_specs=[whole()] * 4,
        out_specs=whole(),
        compiler_params=pltpu.CompilerParams(vmem_limit_bytes=VMEM_LIMIT),
        name="chain",
    )(hall, contact[:, 0], hop, bond)
    table = pltpu.VMEM((row_count, columns, 2, depth, size), F32)
    summed, density = pl.pallas_call(
        functools.partial(phonon_kernel, columns),
        out_shape=(block, jax.ShapeDtypeStruct((1, size), F32)),
        in_specs=[scalar(), scalar(), whole()],
        out_specs=(whole(), whole()),
        scratch_shapes=[table, table, pltpu.VMEM((columns, 8, size), F32)]
        + [dma((columns,))] * 6,
        compiler_params=pltpu.CompilerParams(
            collective_id=1, has_side_effects=True, vmem_limit_bytes=VMEM_LIMIT
        ),
        name="phonon_sum",
    )(shifts, strength, green)
    self_energy = pl.pallas_call(
        coupling_kernel,
        out_shape=block,
        in_specs=[whole()] * 2,
        out_specs=whole(),
        compiler_params=pltpu.CompilerParams(vmem_limit_bytes=VMEM_LIMIT),
        name="coupling",
    )(summed, coupling)
    return (green[:, None, None], self_energy[:, None, None], density)


def solution(mesh):
    in_specs = (
        P("slab", None, None, None),
        P(None, "energy", None, None, None, None),
        P(),
        P(),
        P(),
        P(),
        P(),
    )
    out_specs = (
        P(None, "energy", "slab", None, None, None),
        P(None, "energy", "slab", None, None, None),
        P("slab", None),
    )
    return jax.shard_map(
        functools.partial(per_device, mesh.shape["slab"], mesh.shape["energy"]),
        mesh=mesh, in_specs=in_specs, out_specs=out_specs, check_vma=False,
    )
```

```python
import functools
import math

import jax
import jax.numpy as jnp
from jax import lax
from jax.experimental import pallas as pl
from jax.experimental.pallas import tpu as pltpu
from jax.sharding import PartitionSpec as P

KMAX = 3
BROADENING = 0.5
ENERGY_LOW = 4.0
ENERGY_SPAN = 1.0
MESH = pl.DeviceIdType.MESH
VMEM_LIMIT = 56 * 1024 * 1024
F32 = jnp.float32
BF16 = jnp.bfloat16


def iotas(shape):
    return (
        lax.broadcasted_iota(jnp.int32, shape, 0),
        lax.broadcasted_iota(jnp.int32, shape, 1),
    )


def split(x):
    high = x.astype(BF16)
    return high, (x - high.astype(F32)).astype(BF16)


def dot(a, b):
    return jnp.dot(a, b, preferred_element_type=F32)


def product(a, b):
    size = a[0].shape[-1]
    ar, al = split(a[0])
    ai, am = split(a[1])
    br, bl = split(b[0])
    bi, bm = split(b[1])
    left = jnp.concatenate([ar, al, ar, ai, am, ai], axis=1)
    real = jnp.concatenate([br, br, bl, -bi, -bi, -bm], axis=0)
    imag = jnp.concatenate([bi, bi, bm, br, br, bl], axis=0)
    return dot(left, real), dot(left, imag)


def invert(x):
    size = x[0].shape[-1]
    rows, cols = iotas((size, size))
    eye = rows == cols
    out = []
    recips = []
    for axis in (0, 1):
        dr = jnp.sum(jnp.where(eye, x[0], 0.0), axis=axis, keepdims=True)
        di = jnp.sum(jnp.where(eye, x[1], 0.0), axis=axis, keepdims=True)
        modulus = dr * dr + di * di
        recips.append((dr / modulus, -di / modulus))
    (cr, ci), (rr, ri) = recips
    pr = x[0] * cr - x[1] * ci
    pi = x[0] * ci + x[1] * cr
    qr = jnp.where(eye, 2.0, 0.0) - pr
    qi = -pi
    first = (rr * qr - ri * qi, rr * qi + ri * qr)
    yr, yi = product(x, first)
    return product(first, (jnp.where(eye, 2.0, 0.0) - yr, -yi))


def conjugate(x, coupler):
    left, right, scale_col, scale_row = coupler
    size = left.shape[0]
    hr, lr = split(x[0])
    hi, li = split(x[1])
    moved = dot(left, jnp.concatenate([hr, hi, lr, li], axis=1)).astype(BF16)
    stacked = jnp.concatenate([moved[:, i * size : (i + 1) * size] for i in range(4)], axis=0)
    full = dot(stacked, right)
    real = (full[:size] + full[2 * size : 3 * size]) * scale_col * scale_row
    imag = (full[size : 2 * size] + full[3 * size :]) * scale_col * scale_row
    return real, imag


def born_kernel(
    slabs, columns, ham_ref, contact_ref, hop_ref, bond_ref, shifts_ref, strength_ref,
    coupling_ref, green_ref, summed_ref, density_ref, hall, taken, mixed, shares,
    send_z, recv_z, send_h, recv_h, send1, recv1, send2, recv2, send3, recv3,
):
    column = lax.axis_index("energy")
    slab = lax.axis_index("slab")
    row_count = contact_ref.shape[0]
    size = ham_ref.shape[-1]
    depth = size // columns
    count = row_count * columns
    half = slabs // 2
    last = slabs - 1
    span = range(row_count)
    others = range(1, columns)
    is_left = slab < half
    rows, cols = iotas((size, size))
    eye = rows == cols

    def partner(dc):
        return lax.rem(column + dc + columns, columns)

    def part(index):
        return pl.ds(pl.multiple_of(index * depth, depth), depth)

    def copy(source, target, send, recv, device):
        return pltpu.make_async_remote_copy(
            src_ref=source, dst_ref=target, send_sem=send, recv_sem=recv,
            device_id=device, device_id_type=MESH,
        )

    barrier = pltpu.get_barrier_semaphore()
    for dz in range(1, slabs):
        pl.semaphore_signal(
            barrier, inc=1, device_id=(column, lax.rem(slab + dz, slabs)), device_id_type=MESH
        )
    for dc in others:
        pl.semaphore_signal(barrier, inc=1, device_id=(partner(dc), slab), device_id_type=MESH)
    hall[slab] = jnp.where(rows <= cols, ham_ref[0], ham_ref[1])
    pl.semaphore_wait(barrier, slabs - 1 + columns - 1)

    def along(target):
        piece = hall.at[slab, part(column)]
        return copy(piece, piece, send_z.at[target], recv_z.at[slab], (column, target))

    def along_in(source):
        piece = hall.at[source, part(column)]
        return copy(piece, piece, send_z.at[source], recv_z.at[source], (column, source))

    def across(source, dc):
        piece = hall.at[source, part(column)]
        return copy(
            piece, piece, send_h.at[source, dc], recv_h.at[source, dc], (partner(dc), slab)
        )

    def across_in(source, dc):
        other = partner(-dc)
        piece = hall.at[source, part(other)]
        return copy(piece, piece, send_h.at[source, dc], recv_h.at[source, dc], (other, slab))

    for target in range(slabs):
        @pl.when(slab != target)
        def _():
            along(target).start()

    def choose(left, right):
        return jnp.where(is_left, left, right)

    def coupler(k, down):
        bond = bond_ref[pl.ds(k, 1), :]
        hop_row = hop_ref[pl.ds(k, 1), :]
        hop_col = jnp.sum(jnp.where(eye, hop_row, 0.0), axis=1, keepdims=True)
        turned = jnp.where(rows == bond, 1.0, 0.0).astype(F32)
        plain = turned.T
        moved_col = jnp.sum(turned * hop_row, axis=1, keepdims=True)
        moved_row = jnp.sum(plain * hop_col, axis=0, keepdims=True)
        flag = down.astype(F32)
        left = (flag * turned + (1.0 - flag) * plain).astype(BF16)
        right = (flag * plain + (1.0 - flag) * turned).astype(BF16)
        scales = (jnp.where(down, moved_col, hop_col), jnp.where(down, moved_row, hop_row))
        reverse = (jnp.where(down, hop_col, moved_col), jnp.where(down, hop_row, moved_row))
        return (left, right) + scales, (right, left) + reverse

    near_side, near_back = coupler(choose(0, last - 1), is_left)
    far_side, _ = coupler(choose(last - 1, 0), jnp.logical_not(is_left))
    cross_side, _ = coupler(half - 1, jnp.logical_not(is_left))

    order = [0, last] + list(range(1, last))
    for source in order:
        @pl.when(slab != source)
        def _():
            along_in(source).wait_recv()
            for dc in others:
                across(source, dc).start()

    def arrive(source, wanted):
        @pl.when(jnp.logical_and(slab != source, wanted))
        def _():
            for dc in others:
                across_in(source, dc).wait_recv()

    def onsite(index):
        packed = hall[index]
        turned = packed.T
        real = jnp.where(rows <= cols, packed, turned)
        imag = jnp.where(rows > cols, packed, jnp.where(rows < cols, -turned, 0.0))
        return real, imag

    def base(r, ham):
        position = (r * columns + column).astype(F32)
        energy = ENERGY_LOW + ENERGY_SPAN * position / count
        return (
            jnp.where(eye, energy, 0.0) - ham[0],
            jnp.where(eye, BROADENING, 0.0) - ham[1],
        )

    def minus(a, b):
        return a[0] - b[0], a[1] - b[1]

    def end_inverses(index, end):
        ham = onsite(index)
        return [
            invert(minus(base(r, ham), (contact_ref[r, end, 0], contact_ref[r, end, 1])))
            for r in span
        ]

    is_right = jnp.logical_not(is_left)
    arrive(0, is_left)
    arrive(last, is_right)
    near = end_inverses(choose(0, last), choose(0, 1))
    arrive(0, is_right)
    arrive(last, is_left)
    far = end_inverses(choose(last, 0), choose(1, 0))
    for source in range(1, last):
        arrive(source, slab >= 0)
    mid_ham = onsite(choose(half - 1, half))
    cross_ham = onsite(choose(half, half - 1))

    def outward(r, dc):
        other = partner(dc)
        return copy(
            green_ref.at[r, :, part(other), :], taken.at[r * columns + column],
            send1.at[r, dc], recv1.at[r, dc], (other, slab),
        )

    def outward_in(r, dc):
        other = partner(-dc)
        return copy(
            green_ref.at[r, :, part(other), :], taken.at[r * columns + other],
            send1.at[r, dc], recv1.at[r, dc], (other, slab),
        )

    for r in span:
        opposite = invert(minus(base(r, cross_ham), conjugate(far[r], far_side)))
        reduced = minus(base(r, mid_ham), conjugate(near[r], near_side))
        middle = invert(minus(reduced, conjugate(opposite, cross_side)))
        green_ref[r, 0] = middle[0]
        green_ref[r, 1] = middle[1]

        @pl.when(jnp.logical_or(slab == 0, slab == last))
        def _():
            inner = conjugate((green_ref[r, 0], green_ref[r, 1]), near_back)
            change = product(product(near[r], inner), near[r])
            green_ref[r, 0] = near[r][0] + change[0]
            green_ref[r, 1] = near[r][1] + change[1]

        for dc in others:
            outward(r, dc).start()
        taken[r * columns + column] = green_ref[r, :, part(column), :]

    weights = {}
    for d in range(-KMAX, KMAX + 1):
        if d != 0:
            weights[d] = sum(
                jnp.where(shifts_ref[m] == d, strength_ref[m], 0.0)
                for m in range(shifts_ref.shape[0])
            )
    high, low = split(coupling_ref[...].T)
    right = jnp.concatenate([high, high, low], axis=0)

    def mix(target):
        pieces = []
        for r in span:
            place = r * columns + target
            total = jnp.zeros((2, depth, size), F32)
            for d, weight in weights.items():
                inside = jnp.logical_and(place + d >= 0, place + d < count)
                index = jnp.clip(place + d, 0, count - 1)
                total = total + jnp.where(inside, weight, 0.0) * taken[index]
            pieces.append(total.reshape(2 * depth, size))
        a, b = split(jnp.concatenate(pieces, axis=0))
        moved = dot(jnp.concatenate([a, b, a], axis=1), right)
        return moved.reshape(row_count, 2, depth, size)

    def homeward(dc):
        return copy(
            mixed.at[dc], summed_ref.at[:, :, part(column), :],
            send2.at[dc], recv2.at[dc], (partner(dc), slab),
        )

    def homeward_in(dc):
        other = partner(-dc)
        return copy(
            mixed.at[dc], summed_ref.at[:, :, part(other), :],
            send2.at[dc], recv2.at[dc], (other, slab),
        )

    def share(dc):
        piece = shares.at[column]
        return copy(piece, piece, send3.at[dc], recv3.at[dc], (partner(dc), slab))

    def share_in(dc):
        other = partner(-dc)
        piece = shares.at[other]
        return copy(piece, piece, send3.at[dc], recv3.at[dc], (other, slab))

    for r in span:
        for dc in others:
            outward_in(r, dc).wait_recv()
    for dc in others:
        mixed[dc] = mix(partner(dc))
        homeward(dc).start()

    levels = jnp.zeros((depth, size), F32)
    for e in range(count):
        energy = ENERGY_LOW + ENERGY_SPAN * e / count
        occupation = 1.0 / (1.0 + math.exp(3.0 * (energy - (ENERGY_LOW + 0.5 * ENERGY_SPAN))))
        levels = levels - occupation * taken[e, 1]
    local_rows, local_cols = iotas((depth, size))
    diagonal = jnp.where(local_rows + column * depth == local_cols, levels, 0.0)
    own_share = jnp.sum(diagonal, axis=0, keepdims=True)
    shares[column] = jnp.broadcast_to(own_share, (8, size))
    for dc in others:
        share(dc).start()

    summed_ref[:, :, part(column), :] = mix(column)
    for dc in others:
        share_in(dc).wait_recv()
    density_ref[...] = jnp.sum(shares[...], axis=0)[:1]
    for dc in others:
        homeward_in(dc).wait_recv()
    for target in range(slabs):
        @pl.when(slab != target)
        def _():
            along(target).wait_send()
            for dc in others:
                across(target, dc).wait_send()
    for dc in others:
        for r in span:
            outward(r, dc).wait_send()
        homeward(dc).wait_send()
        share(dc).wait_send()


def coupling_kernel(summed_ref, coupling_ref, green_in, out_ref, green_out, sem):
    through = pltpu.make_async_copy(green_in, green_out, sem)
    through.start()
    high, low = split(coupling_ref[...])
    left = jnp.concatenate([high, low, high], axis=1)
    for r in range(summed_ref.shape[0]):
        for part in range(2):
            a, b = split(summed_ref[r, part])
            out_ref[r, part] = dot(left, jnp.concatenate([a, a, b], axis=0))
    through.wait()


def whole():
    return pl.BlockSpec(memory_space=pltpu.VMEM)


def scalar():
    return pl.BlockSpec(memory_space=pltpu.SMEM)


def anywhere():
    return pl.BlockSpec(memory_space=pl.ANY)


def per_device(slabs, columns, hamiltonian, contact, hop, bond, shifts, strength, coupling):
    size = hamiltonian.shape[-1]
    row_count = contact.shape[0]
    depth = size // columns
    dma = pltpu.SemaphoreType.DMA
    block = jax.ShapeDtypeStruct((row_count, 2, size, size), F32)
    green, summed, density = pl.pallas_call(
        functools.partial(born_kernel, slabs, columns),
        out_shape=(block, block, jax.ShapeDtypeStruct((1, size), F32)),
        in_specs=[whole()] * 4 + [scalar()] * 2 + [whole()],
        out_specs=(whole(),) * 3,
        scratch_shapes=[
            pltpu.VMEM((slabs, size, size), F32),
            pltpu.VMEM((row_count * columns, 2, depth, size), F32),
            pltpu.VMEM((columns, row_count, 2, depth, size), F32),
            pltpu.VMEM((columns, 8, size), F32),
            dma((slabs,)), dma((slabs,)),
            dma((slabs, columns)), dma((slabs, columns)),
            dma((row_count, columns)), dma((row_count, columns)),
            dma((columns,)), dma((columns,)), dma((columns,)), dma((columns,)),
        ],
        compiler_params=pltpu.CompilerParams(
            collective_id=0, has_side_effects=True, vmem_limit_bytes=VMEM_LIMIT
        ),
        name="born",
    )(hamiltonian[0], contact[:, 0], hop, bond, shifts, strength, coupling)
    self_energy, green = pl.pallas_call(
        coupling_kernel,
        out_shape=(block, block),
        in_specs=[whole(), whole(), anywhere()],
        out_specs=(whole(), anywhere()),
        scratch_shapes=[dma],
        compiler_params=pltpu.CompilerParams(vmem_limit_bytes=VMEM_LIMIT),
        name="coupling",
    )(summed, coupling, green)
    return (green[:, None, None], self_energy[:, None, None], density)


def solution(mesh):
    in_specs = (
        P("slab", None, None, None),
        P(None, "energy", None, None, None, None),
        P(),
        P(),
        P(),
        P(),
        P(),
    )
    out_specs = (
        P(None, "energy", "slab", None, None, None),
        P(None, "energy", "slab", None, None, None),
        P("slab", None),
    )
    return jax.shard_map(
        functools.partial(per_device, mesh.shape["slab"], mesh.shape["energy"]),
        mesh=mesh, in_specs=in_specs, out_specs=out_specs, check_vma=False,
    )
```

```python
import functools
import math

import jax
import jax.numpy as jnp
from jax import lax
from jax.experimental import pallas as pl
from jax.experimental.pallas import tpu as pltpu
from jax.sharding import PartitionSpec as P

KMAX = 3
BROADENING = 0.5
ENERGY_LOW = 4.0
ENERGY_SPAN = 1.0
MESH = pl.DeviceIdType.MESH
VMEM_LIMIT = 56 * 1024 * 1024
F32 = jnp.float32
BF16 = jnp.bfloat16


def iotas(shape):
    return (
        lax.broadcasted_iota(jnp.int32, shape, 0),
        lax.broadcasted_iota(jnp.int32, shape, 1),
    )


def split(x):
    high = x.astype(BF16)
    return high, (x - high.astype(F32)).astype(BF16)


def dot(a, b):
    return jnp.dot(a, b, preferred_element_type=F32)


def product(a, b):
    size = a[0].shape[-1]
    ar, al = split(a[0])
    ai, am = split(a[1])
    br, bl = split(b[0])
    bi, bm = split(b[1])
    left = jnp.concatenate(
        [jnp.concatenate([ar, ai], axis=1), jnp.concatenate([al, am], axis=1)], axis=0
    )
    high = jnp.concatenate(
        [jnp.concatenate([br, bi], axis=1), jnp.concatenate([-bi, br], axis=1)], axis=0
    )
    low = jnp.concatenate(
        [jnp.concatenate([bl, bm], axis=1), jnp.concatenate([-bm, bl], axis=1)], axis=0
    )
    full = dot(left, high)
    both = full[:size] + (full[size:] + dot(left[:size], low))
    return both[:, :size], both[:, size:]


def invert(x):
    size = x[0].shape[-1]
    rows, cols = iotas((size, size))
    eye = rows == cols
    out = []
    recips = []
    for axis in (0, 1):
        dr = jnp.sum(jnp.where(eye, x[0], 0.0), axis=axis, keepdims=True)
        di = jnp.sum(jnp.where(eye, x[1], 0.0), axis=axis, keepdims=True)
        modulus = dr * dr + di * di
        recips.append((dr / modulus, -di / modulus))
    (cr, ci), (rr, ri) = recips
    pr = x[0] * cr - x[1] * ci
    pi = x[0] * ci + x[1] * cr
    qr = jnp.where(eye, 2.0, 0.0) - pr
    qi = -pi
    first = (rr * qr - ri * qi, rr * qi + ri * qr)
    yr, yi = product(x, first)
    return product(first, (jnp.where(eye, 2.0, 0.0) - yr, -yi))


def conjugate(x, coupler):
    left, right, scale_col, scale_row = coupler
    size = left.shape[0]
    hr, lr = split(x[0])
    hi, li = split(x[1])
    moved = dot(left, jnp.concatenate([hr, hi, lr, li], axis=1)).astype(BF16)
    stacked = jnp.concatenate([moved[:, i * size : (i + 1) * size] for i in range(4)], axis=0)
    full = dot(stacked, right)
    real = (full[:size] + full[2 * size : 3 * size]) * scale_col * scale_row
    imag = (full[size : 2 * size] + full[3 * size :]) * scale_col * scale_row
    return real, imag


def born_kernel(
    slabs, columns, ham_ref, contact_hbm, hop_ref, bond_ref, shifts_ref, strength_ref,
    coupling_ref, green_ref, summed_ref, density_ref, contact_ref, contact_sem, hall, taken, mixed, shares,
    send_z, recv_z, send_h, recv_h, send1, recv1, send2, recv2, send3, recv3,
):
    column = lax.axis_index("energy")
    slab = lax.axis_index("slab")
    row_count = contact_ref.shape[0]
    size = ham_ref.shape[-1]
    depth = size // columns
    count = row_count * columns
    half = slabs // 2
    last = slabs - 1
    span = range(row_count)
    others = range(1, columns)
    is_left = slab < half
    rows, cols = iotas((size, size))
    eye = rows == cols

    def partner(dc):
        return lax.rem(column + dc + columns, columns)

    def part(index):
        return pl.ds(pl.multiple_of(index * depth, depth), depth)

    def copy(source, target, send, recv, device):
        return pltpu.make_async_remote_copy(
            src_ref=source, dst_ref=target, send_sem=send, recv_sem=recv,
            device_id=device, device_id_type=MESH,
        )

    fetch = pltpu.make_async_copy(contact_hbm, contact_ref, contact_sem)
    fetch.start()

    barrier = pltpu.get_barrier_semaphore()
    for dz in range(1, slabs):
        pl.semaphore_signal(
            barrier, inc=1, device_id=(column, lax.rem(slab + dz, slabs)), device_id_type=MESH
        )
    for dc in others:
        pl.semaphore_signal(barrier, inc=1, device_id=(partner(dc), slab), device_id_type=MESH)
    hall[slab] = jnp.where(rows <= cols, ham_ref[0], ham_ref[1])
    pl.semaphore_wait(barrier, slabs - 1 + columns - 1)

    def along(target):
        piece = hall.at[slab, part(column)]
        return copy(piece, piece, send_z.at[target], recv_z.at[slab], (column, target))

    def along_in(source):
        piece = hall.at[source, part(column)]
        return copy(piece, piece, send_z.at[source], recv_z.at[source], (column, source))

    def across(source, dc):
        piece = hall.at[source, part(column)]
        return copy(
            piece, piece, send_h.at[source, dc], recv_h.at[source, dc], (partner(dc), slab)
        )

    def across_in(source, dc):
        other = partner(-dc)
        piece = hall.at[source, part(other)]
        return copy(piece, piece, send_h.at[source, dc], recv_h.at[source, dc], (other, slab))

    for target in range(slabs):
        @pl.when(slab != target)
        def _():
            along(target).start()

    def choose(left, right):
        return jnp.where(is_left, left, right)

    def coupler(k, down):
        bond = bond_ref[pl.ds(k, 1), :]
        hop_row = hop_ref[pl.ds(k, 1), :]
        hop_col = jnp.sum(jnp.where(eye, hop_row, 0.0), axis=1, keepdims=True)
        turned = jnp.where(rows == bond, 1.0, 0.0).astype(F32)
        plain = turned.T
        moved_col = jnp.sum(turned * hop_row, axis=1, keepdims=True)
        moved_row = jnp.sum(plain * hop_col, axis=0, keepdims=True)
        flag = down.astype(F32)
        left = (flag * turned + (1.0 - flag) * plain).astype(BF16)
        right = (flag * plain + (1.0 - flag) * turned).astype(BF16)
        scales = (jnp.where(down, moved_col, hop_col), jnp.where(down, moved_row, hop_row))
        reverse = (jnp.where(down, hop_col, moved_col), jnp.where(down, hop_row, moved_row))
        return (left, right) + scales, (right, left) + reverse

    near_side, near_back = coupler(choose(0, last - 1), is_left)
    far_side, _ = coupler(choose(last - 1, 0), jnp.logical_not(is_left))
    cross_side, _ = coupler(half - 1, jnp.logical_not(is_left))

    order = [0, last] + list(range(1, last))
    for source in order:
        @pl.when(slab != source)
        def _():
            along_in(source).wait_recv()
            for dc in others:
                across(source, dc).start()

    def arrive(source, wanted):
        @pl.when(jnp.logical_and(slab != source, wanted))
        def _():
            for dc in others:
                across_in(source, dc).wait_recv()

    def onsite(index):
        packed = hall[index]
        turned = packed.T
        real = jnp.where(rows <= cols, packed, turned)
        imag = jnp.where(rows > cols, packed, jnp.where(rows < cols, -turned, 0.0))
        return real, imag

    def base(r, ham):
        position = (r * columns + column).astype(F32)
        energy = ENERGY_LOW + ENERGY_SPAN * position / count
        return (
            jnp.where(eye, energy, 0.0) - ham[0],
            jnp.where(eye, BROADENING, 0.0) - ham[1],
        )

    def minus(a, b):
        return a[0] - b[0], a[1] - b[1]

    def end_inverses(index, end):
        ham = onsite(index)
        return [
            invert(minus(base(r, ham), (contact_ref[r, end, 0], contact_ref[r, end, 1])))
            for r in span
        ]

    is_right = jnp.logical_not(is_left)
    fetch.wait()
    arrive(0, is_left)
    arrive(last, is_right)
    near = end_inverses(choose(0, last), choose(0, 1))
    arrive(0, is_right)
    arrive(last, is_left)
    far = end_inverses(choose(last, 0), choose(1, 0))
    for source in range(1, last):
        arrive(source, slab >= 0)
    mid_ham = onsite(choose(half - 1, half))
    cross_ham = onsite(choose(half, half - 1))

    def outward(r, dc):
        other = partner(dc)
        return copy(
            green_ref.at[r, :, part(other), :], taken.at[r * columns + column],
            send1.at[r, dc], recv1.at[r, dc], (other, slab),
        )

    def outward_in(r, dc):
        other = partner(-dc)
        return copy(
            green_ref.at[r, :, part(other), :], taken.at[r * columns + other],
            send1.at[r, dc], recv1.at[r, dc], (other, slab),
        )

    for r in span:
        opposite = invert(minus(base(r, cross_ham), conjugate(far[r], far_side)))
        reduced = minus(base(r, mid_ham), conjugate(near[r], near_side))
        middle = invert(minus(reduced, conjugate(opposite, cross_side)))
        green_ref[r, 0] = middle[0]
        green_ref[r, 1] = middle[1]

        @pl.when(jnp.logical_or(slab == 0, slab == last))
        def _():
            inner = conjugate((green_ref[r, 0], green_ref[r, 1]), near_back)
            change = product(product(near[r], inner), near[r])
            green_ref[r, 0] = near[r][0] + change[0]
            green_ref[r, 1] = near[r][1] + change[1]

        for dc in others:
            outward(r, dc).start()
        taken[r * columns + column] = green_ref[r, :, part(column), :]

    weights = {}
    for d in range(-KMAX, KMAX + 1):
        if d != 0:
            weights[d] = sum(
                jnp.where(shifts_ref[m] == d, strength_ref[m], 0.0)
                for m in range(shifts_ref.shape[0])
            )
    high, low = split(coupling_ref[...].T)
    right = jnp.concatenate([high, high, low], axis=0)

    def mix(target):
        pieces = []
        for r in span:
            place = r * columns + target
            total = jnp.zeros((2, depth, size), F32)
            for d, weight in weights.items():
                inside = jnp.logical_and(place + d >= 0, place + d < count)
                index = jnp.clip(place + d, 0, count - 1)
                total = total + jnp.where(inside, weight, 0.0) * taken[index]
            pieces.append(total.reshape(2 * depth, size))
        a, b = split(jnp.concatenate(pieces, axis=0))
        moved = dot(jnp.concatenate([a, b, a], axis=1), right)
        return moved.reshape(row_count, 2, depth, size)

    def homeward(dc):
        return copy(
            mixed.at[dc], summed_ref.at[:, :, part(column), :],
            send2.at[dc], recv2.at[dc], (partner(dc), slab),
        )

    def homeward_in(dc):
        other = partner(-dc)
        return copy(
            mixed.at[dc], summed_ref.at[:, :, part(other), :],
            send2.at[dc], recv2.at[dc], (other, slab),
        )

    def share(dc):
        piece = shares.at[column]
        return copy(piece, piece, send3.at[dc], recv3.at[dc], (partner(dc), slab))

    def share_in(dc):
        other = partner(-dc)
        piece = shares.at[other]
        return copy(piece, piece, send3.at[dc], recv3.at[dc], (other, slab))

    for r in span:
        for dc in others:
            outward_in(r, dc).wait_recv()
    for dc in others:
        mixed[dc] = mix(partner(dc))
        homeward(dc).start()

    levels = jnp.zeros((depth, size), F32)
    for e in range(count):
        energy = ENERGY_LOW + ENERGY_SPAN * e / count
        occupation = 1.0 / (1.0 + math.exp(3.0 * (energy - (ENERGY_LOW + 0.5 * ENERGY_SPAN))))
        levels = levels - occupation * taken[e, 1]
    local_rows, local_cols = iotas((depth, size))
    diagonal = jnp.where(local_rows + column * depth == local_cols, levels, 0.0)
    own_share = jnp.sum(diagonal, axis=0, keepdims=True)
    shares[column] = jnp.broadcast_to(own_share, (8, size))
    for dc in others:
        share(dc).start()

    summed_ref[:, :, part(column), :] = mix(column)
    for dc in others:
        share_in(dc).wait_recv()
    density_ref[...] = jnp.sum(shares[...], axis=0)[:1]
    for dc in others:
        homeward_in(dc).wait_recv()
    for target in range(slabs):
        @pl.when(slab != target)
        def _():
            along(target).wait_send()
            for dc in others:
                across(target, dc).wait_send()
    for dc in others:
        for r in span:
            outward(r, dc).wait_send()
        homeward(dc).wait_send()
        share(dc).wait_send()


def coupling_kernel(
    summed_ref, coupling_ref, density_in, green_in, out_ref, density_out, green_out, sem
):
    through = pltpu.make_async_copy(green_in, green_out, sem)
    through.start()
    density_out[...] = density_in[...]
    high, low = split(coupling_ref[...])
    left = jnp.concatenate([high, low, high], axis=1)
    for r in range(summed_ref.shape[0]):
        for part in range(2):
            a, b = split(summed_ref[r, part])
            out_ref[r, part] = dot(left, jnp.concatenate([a, a, b], axis=0))
    through.wait()


def whole():
    return pl.BlockSpec(memory_space=pltpu.VMEM)


def scalar():
    return pl.BlockSpec(memory_space=pltpu.SMEM)


def anywhere():
    return pl.BlockSpec(memory_space=pl.ANY)


def per_device(slabs, columns, hamiltonian, contact, hop, bond, shifts, strength, coupling):
    size = hamiltonian.shape[-1]
    row_count = contact.shape[0]
    depth = size // columns
    dma = pltpu.SemaphoreType.DMA
    block = jax.ShapeDtypeStruct((row_count, 2, size, size), F32)
    green, summed, density = pl.pallas_call(
        functools.partial(born_kernel, slabs, columns),
        out_shape=(block, block, jax.ShapeDtypeStruct((1, size), F32)),
        in_specs=[whole(), anywhere(), whole(), whole(), scalar(), scalar(), whole()],
        out_specs=(whole(),) * 3,
        scratch_shapes=[
            pltpu.VMEM((row_count, 2, 2, size, size), F32),
            dma,
            pltpu.VMEM((slabs, size, size), F32),
            pltpu.VMEM((row_count * columns, 2, depth, size), F32),
            pltpu.VMEM((columns, row_count, 2, depth, size), F32),
            pltpu.VMEM((columns, 8, size), F32),
            dma((slabs,)), dma((slabs,)),
            dma((slabs, columns)), dma((slabs, columns)),
            dma((row_count, columns)), dma((row_count, columns)),
            dma((columns,)), dma((columns,)), dma((columns,)), dma((columns,)),
        ],
        compiler_params=pltpu.CompilerParams(
            collective_id=0, has_side_effects=True, vmem_limit_bytes=VMEM_LIMIT
        ),
        name="born",
    )(hamiltonian[0], contact[:, 0], hop, bond, shifts, strength, coupling)
    self_energy, density, green = pl.pallas_call(
        coupling_kernel,
        out_shape=(block, jax.ShapeDtypeStruct((1, size), F32), block),
        in_specs=[whole()] * 4,
        out_specs=(whole(), whole(), anywhere()),
        scratch_shapes=[dma],
        compiler_params=pltpu.CompilerParams(vmem_limit_bytes=VMEM_LIMIT),
        name="coupling",
    )(summed, coupling, density, green)
    return (green[:, None, None], self_energy[:, None, None], density)


def solution(mesh):
    in_specs = (
        P("slab", None, None, None),
        P(None, "energy", None, None, None, None),
        P(),
        P(),
        P(),
        P(),
        P(),
    )
    out_specs = (
        P(None, "energy", "slab", None, None, None),
        P(None, "energy", "slab", None, None, None),
        P("slab", None),
    )
    return jax.shard_map(
        functools.partial(per_device, mesh.shape["slab"], mesh.shape["energy"]),
        mesh=mesh, in_specs=in_specs, out_specs=out_specs, check_vma=False,
    )
```

```python
import functools
import math

import jax
import jax.numpy as jnp
from jax import lax
from jax.experimental import pallas as pl
from jax.experimental.pallas import tpu as pltpu
from jax.sharding import PartitionSpec as P

KMAX = 3
BROADENING = 0.5
ENERGY_LOW = 4.0
ENERGY_SPAN = 1.0
MESH = pl.DeviceIdType.MESH
VMEM_LIMIT = 56 * 1024 * 1024
F32 = jnp.float32
BF16 = jnp.bfloat16


def iotas(shape):
    return (
        lax.broadcasted_iota(jnp.int32, shape, 0),
        lax.broadcasted_iota(jnp.int32, shape, 1),
    )


def split(x):
    high = x.astype(BF16)
    return high, (x - high.astype(F32)).astype(BF16)


def dot(a, b):
    return jnp.dot(a, b, preferred_element_type=F32)


def product(a, b):
    size = a[0].shape[-1]
    ar, al = split(a[0])
    ai, am = split(a[1])
    br, bl = split(b[0])
    bi, bm = split(b[1])
    left = jnp.concatenate(
        [jnp.concatenate([ar, ai], axis=1), jnp.concatenate([al, am], axis=1)], axis=0
    )
    high = jnp.concatenate(
        [jnp.concatenate([br, bi], axis=1), jnp.concatenate([-bi, br], axis=1)], axis=0
    )
    low = jnp.concatenate(
        [jnp.concatenate([bl, bm], axis=1), jnp.concatenate([-bm, bl], axis=1)], axis=0
    )
    full = dot(left, high)
    both = full[:size] + (full[size:] + dot(left[:size], low))
    return both[:, :size], both[:, size:]


def invert(x):
    size = x[0].shape[-1]
    rows, cols = iotas((size, size))
    eye = rows == cols
    out = []
    recips = []
    for axis in (0, 1):
        dr = jnp.sum(jnp.where(eye, x[0], 0.0), axis=axis, keepdims=True)
        di = jnp.sum(jnp.where(eye, x[1], 0.0), axis=axis, keepdims=True)
        modulus = dr * dr + di * di
        recips.append((dr / modulus, -di / modulus))
    (cr, ci), (rr, ri) = recips
    unit = jnp.where(eye, 1.0, 0.0)
    w = (unit - (x[0] * cr - x[1] * ci), -(x[0] * ci + x[1] * cr))
    v = product(w, w)
    t = product(w, v)
    sr = unit + (w[0] + (v[0] + t[0]))
    si = w[1] + (v[1] + t[1])
    return rr * sr - ri * si, rr * si + ri * sr


def conjugate(x, coupler):
    left, right, scale_col, scale_row = coupler
    size = left.shape[0]
    hr, lr = split(x[0])
    hi, li = split(x[1])
    moved = dot(left, jnp.concatenate([hr, hi, lr, li], axis=1)).astype(BF16)
    stacked = jnp.concatenate([moved[:, i * size : (i + 1) * size] for i in range(4)], axis=0)
    full = dot(stacked, right)
    real = (full[:size] + full[2 * size : 3 * size]) * scale_col * scale_row
    imag = (full[size : 2 * size] + full[3 * size :]) * scale_col * scale_row
    return real, imag


def born_kernel(
    slabs, columns, ham_ref, contact_hbm, hop_ref, bond_ref, shifts_ref, strength_ref,
    coupling_ref, green_ref, summed_ref, density_ref, contact_ref, contact_sem, hall, taken, mixed, shares,
    send_z, recv_z, send_h, recv_h, send1, recv1, send2, recv2, send3, recv3,
):
    column = lax.axis_index("energy")
    slab = lax.axis_index("slab")
    row_count = contact_ref.shape[0]
    size = ham_ref.shape[-1]
    depth = size // columns
    count = row_count * columns
    half = slabs // 2
    last = slabs - 1
    span = range(row_count)
    others = range(1, columns)
    is_left = slab < half
    rows, cols = iotas((size, size))
    eye = rows == cols

    def partner(dc):
        return lax.rem(column + dc + columns, columns)

    def part(index):
        return pl.ds(pl.multiple_of(index * depth, depth), depth)

    def copy(source, target, send, recv, device):
        return pltpu.make_async_remote_copy(
            src_ref=source, dst_ref=target, send_sem=send, recv_sem=recv,
            device_id=device, device_id_type=MESH,
        )

    fetch = pltpu.make_async_copy(contact_hbm, contact_ref, contact_sem)
    fetch.start()

    barrier = pltpu.get_barrier_semaphore()
    for dz in range(1, slabs):
        pl.semaphore_signal(
            barrier, inc=1, device_id=(column, lax.rem(slab + dz, slabs)), device_id_type=MESH
        )
    for dc in others:
        pl.semaphore_signal(barrier, inc=1, device_id=(partner(dc), slab), device_id_type=MESH)
    hall[slab] = jnp.where(rows <= cols, ham_ref[0], ham_ref[1])
    pl.semaphore_wait(barrier, slabs - 1 + columns - 1)

    def along(target):
        piece = hall.at[slab, part(column)]
        return copy(piece, piece, send_z.at[target], recv_z.at[slab], (column, target))

    def along_in(source):
        piece = hall.at[source, part(column)]
        return copy(piece, piece, send_z.at[source], recv_z.at[source], (column, source))

    def across(source, dc):
        piece = hall.at[source, part(column)]
        return copy(
            piece, piece, send_h.at[source, dc], recv_h.at[source, dc], (partner(dc), slab)
        )

    def across_in(source, dc):
        other = partner(-dc)
        piece = hall.at[source, part(other)]
        return copy(piece, piece, send_h.at[source, dc], recv_h.at[source, dc], (other, slab))

    for target in range(slabs):
        @pl.when(slab != target)
        def _():
            along(target).start()

    def choose(left, right):
        return jnp.where(is_left, left, right)

    def coupler(k, down):
        bond = bond_ref[pl.ds(k, 1), :]
        hop_row = hop_ref[pl.ds(k, 1), :]
        hop_col = jnp.sum(jnp.where(eye, hop_row, 0.0), axis=1, keepdims=True)
        turned = jnp.where(rows == bond, 1.0, 0.0).astype(F32)
        plain = turned.T
        moved_col = jnp.sum(turned * hop_row, axis=1, keepdims=True)
        moved_row = jnp.sum(plain * hop_col, axis=0, keepdims=True)
        flag = down.astype(F32)
        left = (flag * turned + (1.0 - flag) * plain).astype(BF16)
        right = (flag * plain + (1.0 - flag) * turned).astype(BF16)
        scales = (jnp.where(down, moved_col, hop_col), jnp.where(down, moved_row, hop_row))
        reverse = (jnp.where(down, hop_col, moved_col), jnp.where(down, hop_row, moved_row))
        return (left, right) + scales, (right, left) + reverse

    near_side, near_back = coupler(choose(0, last - 1), is_left)
    far_side, _ = coupler(choose(last - 1, 0), jnp.logical_not(is_left))
    cross_side, _ = coupler(half - 1, jnp.logical_not(is_left))

    order = [0, last] + list(range(1, last))
    for source in order:
        @pl.when(slab != source)
        def _():
            along_in(source).wait_recv()
            for dc in others:
                across(source, dc).start()

    def arrive(source, wanted):
        @pl.when(jnp.logical_and(slab != source, wanted))
        def _():
            for dc in others:
                across_in(source, dc).wait_recv()

    def onsite(index):
        packed = hall[index]
        turned = packed.T
        real = jnp.where(rows <= cols, packed, turned)
        imag = jnp.where(rows > cols, packed, jnp.where(rows < cols, -turned, 0.0))
        return real, imag

    def base(r, ham):
        position = (r * columns + column).astype(F32)
        energy = ENERGY_LOW + ENERGY_SPAN * position / count
        return (
            jnp.where(eye, energy, 0.0) - ham[0],
            jnp.where(eye, BROADENING, 0.0) - ham[1],
        )

    def minus(a, b):
        return a[0] - b[0], a[1] - b[1]

    def end_inverses(index, end):
        ham = onsite(index)
        return [
            invert(minus(base(r, ham), (contact_ref[r, end, 0], contact_ref[r, end, 1])))
            for r in span
        ]

    is_right = jnp.logical_not(is_left)
    fetch.wait()
    arrive(0, is_left)
    arrive(last, is_right)
    near = end_inverses(choose(0, last), choose(0, 1))
    arrive(0, is_right)
    arrive(last, is_left)
    far_ham, far_end = onsite(choose(last, 0)), choose(1, 0)
    for source in range(1, last):
        arrive(source, slab >= 0)
    mid_ham = onsite(choose(half - 1, half))
    cross_ham = onsite(choose(half, half - 1))

    def outward(r, dc):
        other = partner(dc)
        return copy(
            green_ref.at[r, :, part(other), :], taken.at[r * columns + column],
            send1.at[r, dc], recv1.at[r, dc], (other, slab),
        )

    def outward_in(r, dc):
        other = partner(-dc)
        return copy(
            green_ref.at[r, :, part(other), :], taken.at[r * columns + other],
            send1.at[r, dc], recv1.at[r, dc], (other, slab),
        )

    weights = {}
    for d in range(-KMAX, KMAX + 1):
        if d != 0:
            weights[d] = sum(
                jnp.where(shifts_ref[m] == d, strength_ref[m], 0.0)
                for m in range(shifts_ref.shape[0])
            )
    high, low = split(coupling_ref[...].T)
    right = jnp.concatenate([high, high, low], axis=0)

    def mix(r, target):
        place = r * columns + target
        total = jnp.zeros((2, depth, size), F32)
        for d, weight in weights.items():
            inside = jnp.logical_and(place + d >= 0, place + d < count)
            index = jnp.clip(place + d, 0, count - 1)
            total = total + jnp.where(inside, weight, 0.0) * taken[index]
        a, b = split(total.reshape(2 * depth, size))
        moved = dot(jnp.concatenate([a, b, a], axis=1), right)
        return moved.reshape(2, depth, size)

    def homeward(r, dc):
        return copy(
            mixed.at[dc, r], summed_ref.at[r, :, part(column), :],
            send2.at[r, dc], recv2.at[r, dc], (partner(dc), slab),
        )

    def homeward_in(r, dc):
        other = partner(-dc)
        return copy(
            mixed.at[dc, r], summed_ref.at[r, :, part(other), :],
            send2.at[r, dc], recv2.at[r, dc], (other, slab),
        )

    def send_home(r, dc):
        mixed[dc, r] = mix(r, partner(dc))
        homeward(r, dc).start()

    def settle(r):
        for dc in others:
            outward_in(r, dc).wait_recv()
        for dc in others:
            @pl.when(partner(dc) < columns - KMAX)
            def _():
                send_home(r, dc)

    def share(dc):
        piece = shares.at[column]
        return copy(piece, piece, send3.at[dc], recv3.at[dc], (partner(dc), slab))

    def share_in(dc):
        other = partner(-dc)
        piece = shares.at[other]
        return copy(piece, piece, send3.at[dc], recv3.at[dc], (other, slab))

    for r in span:
        far = invert(
            minus(base(r, far_ham), (contact_ref[r, far_end, 0], contact_ref[r, far_end, 1]))
        )
        opposite = invert(minus(base(r, cross_ham), conjugate(far, far_side)))
        reduced = minus(base(r, mid_ham), conjugate(near[r], near_side))
        if r > 0:
            settle(r - 1)
        middle = invert(minus(reduced, conjugate(opposite, cross_side)))
        green_ref[r, 0] = middle[0]
        green_ref[r, 1] = middle[1]

        @pl.when(jnp.logical_or(slab == 0, slab == last))
        def _():
            inner = conjugate((green_ref[r, 0], green_ref[r, 1]), near_back)
            change = product(product(near[r], inner), near[r])
            green_ref[r, 0] = near[r][0] + change[0]
            green_ref[r, 1] = near[r][1] + change[1]

        for dc in others:
            outward(r, dc).start()
        taken[r * columns + column] = green_ref[r, :, part(column), :]

    for dc in others:
        outward_in(row_count - 1, dc).wait_recv()
    for dc in others:
        send_home(row_count - 1, dc)
        for r in range(row_count - 1):
            @pl.when(partner(dc) >= columns - KMAX)
            def _():
                send_home(r, dc)

    levels = jnp.zeros((depth, size), F32)
    for e in range(count):
        energy = ENERGY_LOW + ENERGY_SPAN * e / count
        occupation = 1.0 / (1.0 + math.exp(3.0 * (energy - (ENERGY_LOW + 0.5 * ENERGY_SPAN))))
        levels = levels - occupation * taken[e, 1]
    local_rows, local_cols = iotas((depth, size))
    diagonal = jnp.where(local_rows + column * depth == local_cols, levels, 0.0)
    own_share = jnp.sum(diagonal, axis=0, keepdims=True)
    shares[column] = jnp.broadcast_to(own_share, (8, size))
    for dc in others:
        share(dc).start()

    for r in span:
        summed_ref[r, :, part(column), :] = mix(r, column)
    for dc in others:
        share_in(dc).wait_recv()
    density_ref[...] = jnp.sum(shares[...], axis=0)[:1]
    for dc in others:
        for r in span:
            homeward_in(r, dc).wait_recv()
    for target in range(slabs):
        @pl.when(slab != target)
        def _():
            along(target).wait_send()
            for dc in others:
                across(target, dc).wait_send()
    for dc in others:
        for r in span:
            outward(r, dc).wait_send()
            homeward(r, dc).wait_send()
        share(dc).wait_send()


def coupling_kernel(
    summed_ref, coupling_ref, density_in, green_in, out_ref, density_out, green_out, sem
):
    through = pltpu.make_async_copy(green_in, green_out, sem)
    through.start()
    density_out[...] = density_in[...]
    high, low = split(coupling_ref[...])
    left = jnp.concatenate([high, low, high], axis=1)
    for r in range(summed_ref.shape[0]):
        for part in range(2):
            a, b = split(summed_ref[r, part])
            out_ref[r, part] = dot(left, jnp.concatenate([a, a, b], axis=0))
    through.wait()


def whole():
    return pl.BlockSpec(memory_space=pltpu.VMEM)


def scalar():
    return pl.BlockSpec(memory_space=pltpu.SMEM)


def anywhere():
    return pl.BlockSpec(memory_space=pl.ANY)


def per_device(slabs, columns, hamiltonian, contact, hop, bond, shifts, strength, coupling):
    size = hamiltonian.shape[-1]
    row_count = contact.shape[0]
    depth = size // columns
    dma = pltpu.SemaphoreType.DMA
    block = jax.ShapeDtypeStruct((row_count, 2, size, size), F32)
    green, summed, density = pl.pallas_call(
        functools.partial(born_kernel, slabs, columns),
        out_shape=(block, block, jax.ShapeDtypeStruct((1, size), F32)),
        in_specs=[whole(), anywhere(), whole(), whole(), scalar(), scalar(), whole()],
        out_specs=(whole(),) * 3,
        scratch_shapes=[
            pltpu.VMEM((row_count, 2, 2, size, size), F32),
            dma,
            pltpu.VMEM((slabs, size, size), F32),
            pltpu.VMEM((row_count * columns, 2, depth, size), F32),
            pltpu.VMEM((columns, row_count, 2, depth, size), F32),
            pltpu.VMEM((columns, 8, size), F32),
            dma((slabs,)), dma((slabs,)),
            dma((slabs, columns)), dma((slabs, columns)),
            dma((row_count, columns)), dma((row_count, columns)),
            dma((row_count, columns)), dma((row_count, columns)),
            dma((columns,)), dma((columns,)),
        ],
        compiler_params=pltpu.CompilerParams(
            collective_id=0, has_side_effects=True, vmem_limit_bytes=VMEM_LIMIT
        ),
        name="born",
    )(hamiltonian[0], contact[:, 0], hop, bond, shifts, strength, coupling)
    self_energy, density, green = pl.pallas_call(
        coupling_kernel,
        out_shape=(block, jax.ShapeDtypeStruct((1, size), F32), block),
        in_specs=[whole()] * 4,
        out_specs=(whole(), whole(), anywhere()),
        scratch_shapes=[dma],
        compiler_params=pltpu.CompilerParams(vmem_limit_bytes=VMEM_LIMIT),
        name="coupling",
    )(summed, coupling, density, green)
    return (green[:, None, None], self_energy[:, None, None], density)


def solution(mesh):
    in_specs = (
        P("slab", None, None, None),
        P(None, "energy", None, None, None, None),
        P(),
        P(),
        P(),
        P(),
        P(),
    )
    out_specs = (
        P(None, "energy", "slab", None, None, None),
        P(None, "energy", "slab", None, None, None),
        P("slab", None),
    )
    return jax.shard_map(
        functools.partial(per_device, mesh.shape["slab"], mesh.shape["energy"]),
        mesh=mesh, in_specs=in_specs, out_specs=out_specs, check_vma=False,
    )
```

```python
import functools
import math

import jax
import jax.numpy as jnp
from jax import lax
from jax.experimental import pallas as pl
from jax.experimental.pallas import tpu as pltpu
from jax.sharding import PartitionSpec as P

KMAX = 3
BROADENING = 0.5
ENERGY_LOW = 4.0
ENERGY_SPAN = 1.0
MESH = pl.DeviceIdType.MESH
VMEM_LIMIT = 56 * 1024 * 1024
F32 = jnp.float32
BF16 = jnp.bfloat16


def iotas(shape):
    return (
        lax.broadcasted_iota(jnp.int32, shape, 0),
        lax.broadcasted_iota(jnp.int32, shape, 1),
    )


def split(x):
    high = x.astype(BF16)
    return high, (x - high.astype(F32)).astype(BF16)


def dot(a, b):
    return jnp.dot(a, b, preferred_element_type=F32)


def product(a, b):
    size = a[0].shape[-1]
    ar, al = split(a[0])
    ai, am = split(a[1])
    br, bl = split(b[0])
    bi, bm = split(b[1])
    left = jnp.concatenate(
        [jnp.concatenate([ar, ai], axis=1), jnp.concatenate([al, am], axis=1)], axis=0
    )
    high = jnp.concatenate(
        [jnp.concatenate([br, bi], axis=1), jnp.concatenate([-bi, br], axis=1)], axis=0
    )
    low = jnp.concatenate(
        [jnp.concatenate([bl, bm], axis=1), jnp.concatenate([-bm, bl], axis=1)], axis=0
    )
    full = dot(left, high)
    both = full[:size] + (full[size:] + dot(left[:size], low))
    return both[:, :size], both[:, size:]


def invert(x):
    size = x[0].shape[-1]
    rows, cols = iotas((size, size))
    eye = rows == cols
    out = []
    recips = []
    for axis in (0, 1):
        dr = jnp.sum(jnp.where(eye, x[0], 0.0), axis=axis, keepdims=True)
        di = jnp.sum(jnp.where(eye, x[1], 0.0), axis=axis, keepdims=True)
        modulus = dr * dr + di * di
        recips.append((dr / modulus, -di / modulus))
    (cr, ci), (rr, ri) = recips
    unit = jnp.where(eye, 1.0, 0.0)
    w = (unit - (x[0] * cr - x[1] * ci), -(x[0] * ci + x[1] * cr))
    v = product(w, w)
    t = product(w, v)
    sr = unit + (w[0] + (v[0] + t[0]))
    si = w[1] + (v[1] + t[1])
    return rr * sr - ri * si, rr * si + ri * sr


def conjugate(x, coupler):
    left, right, scale_col, scale_row = coupler
    size = left.shape[0]
    hr, lr = split(x[0])
    hi, li = split(x[1])
    moved = dot(left, jnp.concatenate([hr, hi, lr, li], axis=1)).astype(BF16)
    stacked = jnp.concatenate([moved[:, i * size : (i + 1) * size] for i in range(4)], axis=0)
    full = dot(stacked, right)
    real = (full[:size] + full[2 * size : 3 * size]) * scale_col * scale_row
    imag = (full[size : 2 * size] + full[3 * size :]) * scale_col * scale_row
    return real, imag


def born_kernel(
    slabs, columns, ham_ref, contact_hbm, hop_ref, bond_ref, shifts_ref, strength_ref,
    coupling_ref, green_ref, summed_ref, density_ref, contact_ref, contact_sem, hall, taken, mixed, shares,
    send_z, recv_z, send_h, recv_h, send1, recv1, send2, recv2, send3, recv3,
):
    column = lax.axis_index("energy")
    slab = lax.axis_index("slab")
    row_count = contact_ref.shape[0]
    size = ham_ref.shape[-1]
    depth = size // columns
    count = row_count * columns
    half = slabs // 2
    last = slabs - 1
    span = range(row_count)
    others = range(1, columns)
    is_left = slab < half
    rows, cols = iotas((size, size))
    eye = rows == cols

    def partner(dc):
        return lax.rem(column + dc + columns, columns)

    def part(index):
        return pl.ds(pl.multiple_of(index * depth, depth), depth)

    def copy(source, target, send, recv, device):
        return pltpu.make_async_remote_copy(
            src_ref=source, dst_ref=target, send_sem=send, recv_sem=recv,
            device_id=device, device_id_type=MESH,
        )

    fetch = pltpu.make_async_copy(contact_hbm, contact_ref, contact_sem)
    fetch.start()

    barrier = pltpu.get_barrier_semaphore()
    for dz in range(1, slabs):
        pl.semaphore_signal(
            barrier, inc=1, device_id=(column, lax.rem(slab + dz, slabs)), device_id_type=MESH
        )
    for dc in others:
        pl.semaphore_signal(barrier, inc=1, device_id=(partner(dc), slab), device_id_type=MESH)
    hall[slab] = jnp.where(rows <= cols, ham_ref[0], ham_ref[1])
    pl.semaphore_wait(barrier, slabs - 1 + columns - 1)

    def along(target):
        piece = hall.at[slab, part(column)]
        return copy(piece, piece, send_z.at[target], recv_z.at[slab], (column, target))

    def along_in(source):
        piece = hall.at[source, part(column)]
        return copy(piece, piece, send_z.at[source], recv_z.at[source], (column, source))

    def across(source, dc):
        piece = hall.at[source, part(column)]
        return copy(
            piece, piece, send_h.at[source, dc], recv_h.at[source, dc], (partner(dc), slab)
        )

    def across_in(source, dc):
        other = partner(-dc)
        piece = hall.at[source, part(other)]
        return copy(piece, piece, send_h.at[source, dc], recv_h.at[source, dc], (other, slab))

    for target in range(slabs):
        @pl.when(slab != target)
        def _():
            along(target).start()

    def choose(left, right):
        return jnp.where(is_left, left, right)

    def coupler(k, down):
        bond = bond_ref[pl.ds(k, 1), :]
        hop_row = hop_ref[pl.ds(k, 1), :]
        hop_col = jnp.sum(jnp.where(eye, hop_row, 0.0), axis=1, keepdims=True)
        turned = jnp.where(rows == bond, 1.0, 0.0).astype(F32)
        plain = turned.T
        moved_col = jnp.sum(turned * hop_row, axis=1, keepdims=True)
        moved_row = jnp.sum(plain * hop_col, axis=0, keepdims=True)
        flag = down.astype(F32)
        left = (flag * turned + (1.0 - flag) * plain).astype(BF16)
        right = (flag * plain + (1.0 - flag) * turned).astype(BF16)
        scales = (jnp.where(down, moved_col, hop_col), jnp.where(down, moved_row, hop_row))
        reverse = (jnp.where(down, hop_col, moved_col), jnp.where(down, hop_row, moved_row))
        return (left, right) + scales, (right, left) + reverse

    near_side, near_back = coupler(choose(0, last - 1), is_left)
    far_side, _ = coupler(choose(last - 1, 0), jnp.logical_not(is_left))
    cross_side, _ = coupler(half - 1, jnp.logical_not(is_left))

    order = [0, last] + list(range(1, last))
    for source in order:
        @pl.when(slab != source)
        def _():
            along_in(source).wait_recv()
            for dc in others:
                across(source, dc).start()

    def arrive(source, wanted):
        @pl.when(jnp.logical_and(slab != source, wanted))
        def _():
            for dc in others:
                across_in(source, dc).wait_recv()

    def onsite(index):
        packed = hall[index]
        turned = packed.T
        real = jnp.where(rows <= cols, packed, turned)
        imag = jnp.where(rows > cols, packed, jnp.where(rows < cols, -turned, 0.0))
        return real, imag

    def base(r, ham):
        position = (r * columns + column).astype(F32)
        energy = ENERGY_LOW + ENERGY_SPAN * position / count
        return (
            jnp.where(eye, energy, 0.0) - ham[0],
            jnp.where(eye, BROADENING, 0.0) - ham[1],
        )

    def minus(a, b):
        return a[0] - b[0], a[1] - b[1]

    def end_inverses(index, end):
        ham = onsite(index)
        return [
            invert(minus(base(r, ham), (contact_ref[r, end, 0], contact_ref[r, end, 1])))
            for r in span
        ]

    is_right = jnp.logical_not(is_left)
    fetch.wait()
    arrive(0, is_left)
    arrive(last, is_right)
    near = end_inverses(choose(0, last), choose(0, 1))
    arrive(0, is_right)
    arrive(last, is_left)
    far = end_inverses(choose(last, 0), choose(1, 0))
    for source in range(1, last):
        arrive(source, slab >= 0)
    mid_ham = onsite(choose(half - 1, half))
    cross_ham = onsite(choose(half, half - 1))

    def outward(r, dc):
        other = partner(dc)
        return copy(
            green_ref.at[r, :, part(other), :], taken.at[r * columns + column],
            send1.at[r, dc], recv1.at[r, dc], (other, slab),
        )

    def outward_in(r, dc):
        other = partner(-dc)
        return copy(
            green_ref.at[r, :, part(other), :], taken.at[r * columns + other],
            send1.at[r, dc], recv1.at[r, dc], (other, slab),
        )

    for r in span:
        opposite = invert(minus(base(r, cross_ham), conjugate(far[r], far_side)))
        reduced = minus(base(r, mid_ham), conjugate(near[r], near_side))
        middle = invert(minus(reduced, conjugate(opposite, cross_side)))
        green_ref[r, 0] = middle[0]
        green_ref[r, 1] = middle[1]

        @pl.when(jnp.logical_or(slab == 0, slab == last))
        def _():
            inner = conjugate((green_ref[r, 0], green_ref[r, 1]), near_back)
            change = product(product(near[r], inner), near[r])
            green_ref[r, 0] = near[r][0] + change[0]
            green_ref[r, 1] = near[r][1] + change[1]

        for dc in others:
            outward(r, dc).start()
        taken[r * columns + column] = green_ref[r, :, part(column), :]

    weights = {}
    for d in range(-KMAX, KMAX + 1):
        if d != 0:
            weights[d] = sum(
                jnp.where(shifts_ref[m] == d, strength_ref[m], 0.0)
                for m in range(shifts_ref.shape[0])
            )
    high, low = split(coupling_ref[...].T)
    right = jnp.concatenate([high, high, low], axis=0)

    def mix(target):
        pieces = []
        for r in span:
            place = r * columns + target
            total = jnp.zeros((2, depth, size), F32)
            for d, weight in weights.items():
                inside = jnp.logical_and(place + d >= 0, place + d < count)
                index = jnp.clip(place + d, 0, count - 1)
                total = total + jnp.where(inside, weight, 0.0) * taken[index]
            pieces.append(total.reshape(2 * depth, size))
        a, b = split(jnp.concatenate(pieces, axis=0))
        moved = dot(jnp.concatenate([a, b, a], axis=1), right)
        return moved.reshape(row_count, 2, depth, size)

    def homeward(dc):
        return copy(
            mixed.at[dc], summed_ref.at[:, :, part(column), :],
            send2.at[dc], recv2.at[dc], (partner(dc), slab),
        )

    def homeward_in(dc):
        other = partner(-dc)
        return copy(
            mixed.at[dc], summed_ref.at[:, :, part(other), :],
            send2.at[dc], recv2.at[dc], (other, slab),
        )

    def share(dc):
        piece = shares.at[column]
        return copy(piece, piece, send3.at[dc], recv3.at[dc], (partner(dc), slab))

    def share_in(dc):
        other = partner(-dc)
        piece = shares.at[other]
        return copy(piece, piece, send3.at[dc], recv3.at[dc], (other, slab))

    for r in span:
        for dc in others:
            outward_in(r, dc).wait_recv()
    for dc in others:
        mixed[dc] = mix(partner(dc))
        homeward(dc).start()

    levels = jnp.zeros((depth, size), F32)
    for e in range(count):
        energy = ENERGY_LOW + ENERGY_SPAN * e / count
        occupation = 1.0 / (1.0 + math.exp(3.0 * (energy - (ENERGY_LOW + 0.5 * ENERGY_SPAN))))
        levels = levels - occupation * taken[e, 1]
    local_rows, local_cols = iotas((depth, size))
    diagonal = jnp.where(local_rows + column * depth == local_cols, levels, 0.0)
    own_share = jnp.sum(diagonal, axis=0, keepdims=True)
    shares[column] = jnp.broadcast_to(own_share, (8, size))
    for dc in others:
        share(dc).start()

    summed_ref[:, :, part(column), :] = mix(column)
    for dc in others:
        share_in(dc).wait_recv()
    density_ref[...] = jnp.sum(shares[...], axis=0)[:1]
    for dc in others:
        homeward_in(dc).wait_recv()
    for target in range(slabs):
        @pl.when(slab != target)
        def _():
            along(target).wait_send()
            for dc in others:
                across(target, dc).wait_send()
    for dc in others:
        for r in span:
            outward(r, dc).wait_send()
        homeward(dc).wait_send()
        share(dc).wait_send()


def coupling_kernel(
    summed_ref, coupling_ref, density_in, green_in, out_ref, density_out, green_out, sem
):
    through = pltpu.make_async_copy(green_in, green_out, sem)
    through.start()
    density_out[...] = density_in[...]
    high, low = split(coupling_ref[...])
    left = jnp.concatenate([high, low, high], axis=1)
    for r in range(summed_ref.shape[0]):
        for part in range(2):
            a, b = split(summed_ref[r, part])
            out_ref[r, part] = dot(left, jnp.concatenate([a, a, b], axis=0))
    through.wait()


def whole():
    return pl.BlockSpec(memory_space=pltpu.VMEM)


def scalar():
    return pl.BlockSpec(memory_space=pltpu.SMEM)


def anywhere():
    return pl.BlockSpec(memory_space=pl.ANY)


def per_device(slabs, columns, hamiltonian, contact, hop, bond, shifts, strength, coupling):
    size = hamiltonian.shape[-1]
    row_count = contact.shape[0]
    depth = size // columns
    dma = pltpu.SemaphoreType.DMA
    block = jax.ShapeDtypeStruct((row_count, 2, size, size), F32)
    green, summed, density = pl.pallas_call(
        functools.partial(born_kernel, slabs, columns),
        out_shape=(block, block, jax.ShapeDtypeStruct((1, size), F32)),
        in_specs=[whole(), anywhere(), whole(), whole(), scalar(), scalar(), whole()],
        out_specs=(whole(),) * 3,
        scratch_shapes=[
            pltpu.VMEM((row_count, 2, 2, size, size), F32),
            dma,
            pltpu.VMEM((slabs, size, size), F32),
            pltpu.VMEM((row_count * columns, 2, depth, size), F32),
            pltpu.VMEM((columns, row_count, 2, depth, size), F32),
            pltpu.VMEM((columns, 8, size), F32),
            dma((slabs,)), dma((slabs,)),
            dma((slabs, columns)), dma((slabs, columns)),
            dma((row_count, columns)), dma((row_count, columns)),
            dma((columns,)), dma((columns,)), dma((columns,)), dma((columns,)),
        ],
        compiler_params=pltpu.CompilerParams(
            collective_id=0, has_side_effects=True, vmem_limit_bytes=VMEM_LIMIT
        ),
        name="born",
    )(hamiltonian[0], contact[:, 0], hop, bond, shifts, strength, coupling)
    self_energy, density, green = pl.pallas_call(
        coupling_kernel,
        out_shape=(block, jax.ShapeDtypeStruct((1, size), F32), block),
        in_specs=[whole()] * 4,
        out_specs=(whole(), whole(), anywhere()),
        scratch_shapes=[dma],
        compiler_params=pltpu.CompilerParams(vmem_limit_bytes=VMEM_LIMIT),
        name="coupling",
    )(summed, coupling, density, green)
    return (green[:, None, None], self_energy[:, None, None], density)


def solution(mesh):
    in_specs = (
        P("slab", None, None, None),
        P(None, "energy", None, None, None, None),
        P(),
        P(),
        P(),
        P(),
        P(),
    )
    out_specs = (
        P(None, "energy", "slab", None, None, None),
        P(None, "energy", "slab", None, None, None),
        P("slab", None),
    )
    return jax.shard_map(
        functools.partial(per_device, mesh.shape["slab"], mesh.shape["energy"]),
        mesh=mesh, in_specs=in_specs, out_specs=out_specs, check_vma=False,
    )
```
